32 devices in a mesh: section: 4 (over y, x), row: 4 (over z), col: 2 (over core).
Axes of the slice: x: 2, y: 2, z: 4, core: 2. Of those that a mesh axis runs over, the one named last changes fastest.
Arguments:
- block_input: float32 [4, 4, 256, 16, 256], P('section', None, None, 'row', 'col'), may hold values from -6 to 6
- grad_out: float32 [4, 256, 16, 256], P(None, None, 'row', 'col'), may hold values from -6 to 6
- w_reduce: float32 [4, 256, 64], P('section'), may hold values from -0.375 to 0.375
- w_spatial: float32 [4, 3, 3, 64, 64], P('section'), may hold values from -0.25 to 0.25
- w_expand: float32 [4, 64, 256], P('section'), may hold values from -0.75 to 0.75
- scale_one: float32 [4, 64], P('section'), may hold values from 0.1 to 1.9
- shift_one: float32 [4, 64], P('section'), may hold values from -3 to 3
- scale_two: float32 [4, 64], P('section'), may hold values from 0.1 to 1.9
- shift_two: float32 [4, 64], P('section'), may hold values from -3 to 3
- scale_three: float32 [4, 256], P('section'), may hold values from 0.1 to 1.9
- shift_three: float32 [4, 256], P('section'), may hold values from -3 to 3
Outputs:
- input_grads: float32 [4, 4, 256, 16, 256], P('section', None, None, 'row', 'col')
- reduce_grad: float32 [4, 256, 64], P('section')
- spatial_grad: float32 [4, 3, 3, 64, 64], P('section')
- expand_grad: float32 [4, 64, 256], P('section')
The draws below stay inside these ranges and needn't reach their ends.
All inputs are finite; a program needn't handle non-finite values.
Results may differ from the reference program's by a relative error of at most 0.00026.
Values sent between devices are 32-bit elements; how exact they have to be, the bound alone decides.
A program may use at most 128 MiB of HBM per device.

```python
import jax
import jax.numpy as jnp
from jax import lax

C = 256
M = 64
IMAGES = 4
SECTIONS = 4
ROWS = 16
COLS = 256


def level_of(rng, shape, cuts, smallest, high):
    def one(dim, parts):
        heights = jax.random.uniform(jax.random.fold_in(jax.random.fold_in(rng, 6), dim), (parts,), jnp.float32, smallest / len(cuts), high / len(cuts))
        return jnp.repeat(jnp.exp(heights), shape[dim] // parts).reshape((-1,) + (1,) * (len(shape) - dim - 1))

    gain = one(*cuts[0])
    for cut in cuts[1:]:
        gain = gain * one(*cut)
    return gain


def gaussian(stream_key, dims, width, limit, cuts=(), held_as=jnp.bfloat16):
    result = jax.random.normal(stream_key, dims, jnp.float32) * width
    if len(cuts) > 0:
        result = level_of(stream_key, dims, cuts, -0.22, 0.18) * result
    return jnp.clip(result, min=-limit, max=limit).astype(held_as)


def setup_inputs(seed: int = 0) -> dict:
    splits = jax.random.split(jax.random.key(seed), 12)
    block_input = gaussian(splits[0], (SECTIONS, IMAGES, C, ROWS, COLS), 1.0, 6.0, ((0, 4), (3, 4), (4, 2)), jnp.float32)
    grad_out = gaussian(splits[1], (IMAGES, C, ROWS, COLS), 1.0, 6.0, ((2, 4), (3, 2)), jnp.float32)
    w_reduce = gaussian(splits[2], (SECTIONS, C, M), C ** -0.5, 0.375, ((0, 4),), jnp.float32)
    w_spatial = gaussian(splits[3], (SECTIONS, 3, 3, M, M), (9 * M) ** -0.5, 0.25, ((0, 4),), jnp.float32)
    w_expand = gaussian(splits[4], (SECTIONS, M, C), M ** -0.5, 0.75, ((0, 4),), jnp.float32)
    scale_one = jnp.clip(1.0 + 0.18 * jax.random.normal(splits[5], (SECTIONS, M), jnp.float32), 0.1, 1.9)
    shift_one = gaussian(splits[6], (SECTIONS, M), 0.5, 3.0, ((0, 4),), jnp.float32)
    scale_two = jnp.clip(1.0 + 0.18 * jax.random.normal(splits[7], (SECTIONS, M), jnp.float32), 0.1, 1.9)
    shift_two = gaussian(splits[8], (SECTIONS, M), 0.5, 3.0, ((0, 4),), jnp.float32)
    scale_three = jnp.clip(1.0 + 0.18 * jax.random.normal(splits[9], (SECTIONS, C), jnp.float32), 0.1, 1.9)
    shift_three = gaussian(splits[10], (SECTIONS, C), 0.5, 3.0, ((0, 4),), jnp.float32)
    return dict(block_input=block_input, grad_out=grad_out, w_reduce=w_reduce, w_spatial=w_spatial, w_expand=w_expand, scale_one=scale_one, shift_one=shift_one, scale_two=scale_two, shift_two=shift_two, scale_three=scale_three, shift_three=shift_three)


highest = lax.Precision.HIGHEST

def silu_grad(values):
    sig = jax.nn.sigmoid(values)
    return sig * (1.0 + values * (1.0 - sig))

def pointwise(values, weight):
    return jnp.einsum('nchw,cm->nmhw', values, weight, precision=highest)

def pointwise_back(values, weight):
    return jnp.einsum('nmhw,cm->nchw', values, weight, precision=highest)

def pad_cells(values):
    return jnp.pad(values, ((0, 0), (0, 0), (1, 1), (1, 1)))

def spatial(padded, weight, height, breadth):
    total = jnp.zeros((padded.shape[0], weight.shape[3], height, breadth), jnp.float32)
    for offset_row in range(3):
        for offset_col in range(3):
            piece = padded[:, :, offset_row:offset_row + height, offset_col:offset_col + breadth]
            total = total + pointwise(piece, weight[offset_row, offset_col])
    return total

def spatial_back(padded, weight, height, breadth):
    total = jnp.zeros((padded.shape[0], weight.shape[2], height, breadth), jnp.float32)
    for offset_row in range(3):
        for offset_col in range(3):
            piece = padded[:, :, 2 - offset_row:2 - offset_row + height, 2 - offset_col:2 - offset_col + breadth]
            total = total + pointwise_back(piece, weight[offset_row, offset_col])
    return total

def spatial_weight(padded, grad_second, height, breadth):
    rows_out = []
    for offset_row in range(3):
        cols_out = []
        for offset_col in range(3):
            piece = padded[:, :, offset_row:offset_row + height, offset_col:offset_col + breadth]
            cols_out.append(jnp.einsum('nchw,nohw->co', piece, grad_second, precision=highest))
        rows_out.append(jnp.stack(cols_out))
    return jnp.stack(rows_out)

def per_channel(values):
    return values[:, None, None]

def block_grad(inputs, upstream, w_reduce, w_spatial, w_expand, scale_one, shift_one, scale_two, shift_two, scale_three, shift_three):
    height, breadth = (inputs.shape[2], inputs.shape[3])
    first = pointwise(inputs, w_reduce) * per_channel(scale_one) + per_channel(shift_one)
    hidden_one = jax.nn.silu(first)
    padded_one = pad_cells(hidden_one)
    second = spatial(padded_one, w_spatial, height, breadth) * per_channel(scale_two) + per_channel(shift_two)
    hidden_two = jax.nn.silu(second)
    third = pointwise(hidden_two, w_expand) * per_channel(scale_three) + per_channel(shift_three)
    joined = inputs + third
    grad_joined = upstream * silu_grad(joined)
    grad_third = grad_joined * per_channel(scale_three)
    expand_term = jnp.einsum('nmhw,nchw->mc', hidden_two, grad_third, precision=highest)
    grad_second = pointwise_back(grad_third, w_expand) * silu_grad(second) * per_channel(scale_two)
    spatial_term = spatial_weight(padded_one, grad_second, height, breadth)
    grad_first = spatial_back(pad_cells(grad_second), w_spatial, height, breadth) * silu_grad(first) * per_channel(scale_one)
    reduce_term = jnp.einsum('nchw,nmhw->cm', inputs, grad_first, precision=highest)
    down_grad = grad_joined + pointwise_back(grad_first, w_reduce)
    return (down_grad, reduce_term, spatial_term, expand_term)

def reference(block_input, grad_out, w_reduce, w_spatial, w_expand, scale_one, shift_one, scale_two, shift_two, scale_three, shift_three):
    factor = 1.0 / jnp.sqrt(jnp.float32(IMAGES * ROWS * COLS))
    input_list = [None] * SECTIONS
    reduce_list = [None] * SECTIONS
    spatial_list = [None] * SECTIONS
    expand_list = [None] * SECTIONS
    upstream_all = grad_out
    for section_now in range(SECTIONS - 1, -1, -1):
        outs_down = []
        reduce_sum = jnp.zeros((C, M), jnp.float32)
        spatial_sum = jnp.zeros((3, 3, M, M), jnp.float32)
        expand_sum = jnp.zeros((M, C), jnp.float32)
        for image in range(IMAGES):
            down_grad, reduce_term, spatial_term, expand_term = block_grad(block_input[section_now, image:image + 1], upstream_all[image:image + 1], w_reduce[section_now], w_spatial[section_now], w_expand[section_now], scale_one[section_now], shift_one[section_now], scale_two[section_now], shift_two[section_now], scale_three[section_now], shift_three[section_now])
            outs_down.append(down_grad)
            reduce_sum = reduce_sum + reduce_term
            spatial_sum = spatial_sum + spatial_term
            expand_sum = expand_sum + expand_term
        upstream_all = jnp.concatenate(outs_down, axis=0)
        input_list[section_now] = upstream_all
        reduce_list[section_now] = reduce_sum * factor
        spatial_list[section_now] = spatial_sum * factor
        expand_list[section_now] = expand_sum * factor
    return (jnp.stack(input_list), jnp.stack(reduce_list), jnp.stack(spatial_list), jnp.stack(expand_list))
```

```python
import functools

import jax
import jax.numpy as jnp
from jax import lax
from jax.experimental import pallas as pl
from jax.experimental.pallas import tpu as pltpu
from jax.sharding import PartitionSpec as P

MESH = pl.DeviceIdType.MESH
BF16 = jnp.bfloat16
F32 = jnp.float32

DIRS = [(-1, 0), (1, 0), (-1, -1), (0, -1), (1, -1), (-1, 1), (0, 1), (1, 1)]


def split(value):
    hi = value.astype(BF16)
    lo = (value - hi.astype(F32)).astype(BF16)
    return hi, lo


def dot3(a, b, dims):
    nums = (dims, ((), ()))
    one = lax.dot_general(a[0], b[0], nums, preferred_element_type=F32)
    two = lax.dot_general(a[0], b[1], nums, preferred_element_type=F32)
    three = lax.dot_general(a[1], b[0], nums, preferred_element_type=F32)
    return one + (two + three)


NN = ((1,), (0,))
NT = ((1,), (1,))


def sigmoid(z):
    return 0.5 * jnp.tanh(0.5 * z) + 0.5


def silu_and_grad(z):
    sig = sigmoid(z)
    return z * sig, sig * (1.0 + z * (1.0 - sig))


def kernel(
    sizes,
    x_ref,
    go_ref,
    w1t_ref,
    w1_ref,
    wf_ref,
    wb_ref,
    w3t_ref,
    w3_ref,
    sm_ref,
    sc_ref,
    out_ref,
    rg_ref,
    sg_ref,
    eg_ref,
    up_ref,
    d_ref,
    hp_ref,
    gp_ref,
    hc_ref,
    gc_ref,
    hk_ref,
    gk_ref,
    shi_ref,
    slo_ref,
    thi_ref,
    tlo_ref,
    f1_ref,
    f2_ref,
    h2hi_ref,
    h2lo_ref,
    gj_ref,
    wide_hi,
    wide_lo,
    w1t_s,
    w1_s,
    wf_s,
    wb_s,
    w3t_s,
    w3_s,
    h_send,
    h_recv,
    g_send,
    g_recv,
    r_send,
    r_recv,
    go_sem,
):
    sections, rows, cols, images, height, breadth, chans, mids = sizes
    sec = lax.axis_index("section")
    row = lax.axis_index("row")
    col = lax.axis_index("col")
    span = height * breadth
    is_last = sec == sections - 1

    def inside(dr, dc):
        ok = jnp.bool_(True)
        if dr == -1:
            ok = row > 0
        if dr == 1:
            ok = row < rows - 1
        if dc == -1:
            ok = jnp.logical_and(ok, col > 0)
        if dc == 1:
            ok = jnp.logical_and(ok, col < cols - 1)
        return ok

    def peer(dr, dc):
        return {"row": row + dr, "col": col + dc}

    whole = chans * height

    def image_of(ref, n):
        return ref.at[pl.ds(n * whole, whole)]

    def strided(n, r):
        return pl.ds(n * whole + r, chans, stride=height)

    barrier = pltpu.get_barrier_semaphore()
    count = jnp.int32(0)
    for dr, dc in DIRS:
        ok = inside(dr, dc)
        count = count + ok.astype(jnp.int32)

        @pl.when(ok)
        def _():
            pl.semaphore_signal(barrier, inc=1, device_id=peer(dr, dc), device_id_type=MESH)

    for ds in (-1, 1):
        ok = sec > 0 if ds == -1 else sec < sections - 1
        count = count + ok.astype(jnp.int32)

        @pl.when(ok)
        def _():
            pl.semaphore_signal(
                barrier, inc=1, device_id={"section": sec + ds}, device_id_type=MESH
            )

    @pl.when(is_last)
    def _():
        for n in range(images):
            pltpu.make_async_copy(image_of(go_ref, n), image_of(up_ref, n), go_sem.at[n]).start()

    edge = jnp.zeros((mids, breadth), F32)
    for pad, packed in ((hp_ref, hc_ref), (gp_ref, gc_ref)):

        @pl.when(row == 0)
        def _():
            for n in range(images):
                pad[n, 0] = edge

        @pl.when(row == rows - 1)
        def _():
            for n in range(images):
                pad[n, height + 1] = edge

        for side in range(2):
            for idx in range(3):
                source = inside(idx - 1, -1 if side == 0 else 1)

                @pl.when(jnp.logical_not(source))
                def _():
                    for n in range(images):
                        packed[n, side, idx] = edge

    for src, dst in (
        (w1t_ref, w1t_s),
        (w1_ref, w1_s),
        (wf_ref, wf_s),
        (wb_ref, wb_s),
        (w3t_ref, w3t_s),
        (w3_ref, w3_s),
    ):
        hi, lo = split(src[...])
        dst[0] = hi
        dst[1] = lo

    rg_ref[...] = jnp.zeros_like(rg_ref)
    sg_ref[...] = jnp.zeros_like(sg_ref)
    eg_ref[...] = jnp.zeros_like(eg_ref)

    def weight(ref):
        return ref[0], ref[1]

    s1 = sm_ref[:, 0:1]
    b1 = sm_ref[:, 1:2]
    s2 = sm_ref[:, 2:3]
    b2 = sm_ref[:, 3:4]
    s3 = sc_ref[:, 0:1]
    b3 = sc_ref[:, 1:2]

    pl.semaphore_wait(barrier, count)

    lane = lax.broadcasted_iota(jnp.int32, (mids, breadth), 1)

    def halo_copy(n, i, pad, packed, keep, send, recv, where_to):
        dr, dc = DIRS[i]
        if dc == 0:
            src = pad.at[n, 1 if dr == -1 else height]
            dst = pad.at[n, height + 1 if dr == -1 else 0]
        else:
            src = keep.at[n, 0 if dc == -1 else 1]
            dst = packed.at[n, 1 if dc == -1 else 0, 1 - dr]
        return pltpu.make_async_remote_copy(
            src_ref=src,
            dst_ref=dst,
            send_sem=send.at[n, i],
            recv_sem=recv.at[n, i],
            device_id=peer(dr * where_to, dc * where_to),
            device_id_type=MESH,
        )

    def halo_send(n, pad, packed, keep, send, recv):
        left = jnp.zeros((mids, breadth), F32)
        right = jnp.zeros((mids, breadth), F32)
        for r in range(height):
            value = pad[n, r + 1]
            left = jnp.where(lane == r, value[:, 0:1], left)
            right = jnp.where(lane == r, value[:, breadth - 1 : breadth], right)
        keep[n, 0] = left
        keep[n, 1] = right
        for i, (dr, dc) in enumerate(DIRS):

            @pl.when(inside(dr, dc))
            def _():
                halo_copy(n, i, pad, packed, keep, send, recv, 1).start()

    def halo_wait(n, pad, packed, keep, send, recv):
        for i, (dr, dc) in enumerate(DIRS):

            @pl.when(inside(-dr, -dc))
            def _():
                halo_copy(n, i, pad, packed, keep, send, recv, -1).wait_recv()

    def halo_drain(n, pad, packed, keep, send, recv):
        for i, (dr, dc) in enumerate(DIRS):

            @pl.when(inside(dr, dc))
            def _():
                halo_copy(n, i, pad, packed, keep, send, recv, 1).wait_send()

    h_args = (hp_ref, hc_ref, hk_ref, h_send, h_recv)
    g_args = (gp_ref, gc_ref, gk_ref, g_send, g_recv)

    def stack(n, pad, packed, hi_out, lo_out, order):
        for p in range(height + 2):
            value = pad[n, p]
            if p == 0:
                idx, at = 0, height - 1
            elif p == height + 1:
                idx, at = 2, 0
            else:
                idx, at = 1, p - 1
            before = jnp.where(lane == 0, packed[n, 0, idx][:, at : at + 1], pltpu.roll(value, 1, 1))
            after = jnp.where(
                lane == breadth - 1,
                packed[n, 1, idx][:, at : at + 1],
                pltpu.roll(value, breadth - 1, 1),
            )
            for slot, piece in zip(order, (before, value, after)):
                hi, lo = split(piece)
                hi_out[slot * mids : (slot + 1) * mids, p * breadth : (p + 1) * breadth] = hi
                lo_out[slot * mids : (slot + 1) * mids, p * breadth : (p + 1) * breadth] = lo

    def load_x(n):
        for r in range(height):
            hi, lo = split(x_ref[strided(n, r), :])
            wide_hi[:, r * breadth : (r + 1) * breadth] = hi
            wide_lo[:, r * breadth : (r + 1) * breadth] = lo

    def forward_one(n):
        load_x(n)
        first = dot3(weight(w1t_s), (wide_hi[...], wide_lo[...]), NN) * s1 + b1
        hidden, slope = silu_and_grad(first)
        f1_ref[n] = slope * s1
        for r in range(height):
            hp_ref[n, r + 1] = hidden[:, r * breadth : (r + 1) * breadth]
        halo_send(n, *h_args)

    def forward_two(n):
        halo_wait(n, *h_args)
        stack(n, hp_ref, hc_ref, shi_ref.at[n], slo_ref.at[n], (0, 1, 2))
        taps = dot3(weight(wf_s), (shi_ref[n], slo_ref[n]), NN)
        second = taps[0:mids, 0:span]
        second = second + taps[mids : 2 * mids, breadth : breadth + span]
        second = second + taps[2 * mids : 3 * mids, 2 * breadth : 2 * breadth + span]
        second = second * s2 + b2
        hidden, slope = silu_and_grad(second)
        f2_ref[n] = slope * s2
        hi, lo = split(hidden)
        h2hi_ref[n] = hi
        h2lo_ref[n] = lo
        for r in range(height):
            at = slice(r * breadth, (r + 1) * breadth)
            third = dot3(weight(w3t_s), (hi[:, at], lo[:, at]), NN) * s3 + b3
            joined = x_ref[strided(n, r), :] + third
            d_ref[n, :, at] = silu_and_grad(joined)[1]

    def relay(n, other):
        return pltpu.make_async_remote_copy(
            src_ref=image_of(out_ref, n),
            dst_ref=image_of(up_ref, n),
            send_sem=r_send.at[n],
            recv_sem=r_recv.at[n],
            device_id={"section": other},
            device_id_type=MESH,
        )

    def backward_one(n):
        @pl.when(is_last)
        def _():
            pltpu.make_async_copy(image_of(go_ref, n), image_of(up_ref, n), go_sem.at[n]).wait()

        @pl.when(jnp.logical_not(is_last))
        def _():
            relay(n, sec + 1).wait_recv()

        for r in range(height):
            at = slice(r * breadth, (r + 1) * breadth)
            joined = up_ref[strided(n, r), :] * d_ref[n, :, at]
            gj_ref[:, at] = joined
            hi, lo = split(joined * s3)
            wide_hi[:, at] = hi
            wide_lo[:, at] = lo
        wide = (wide_hi[...], wide_lo[...])
        second = dot3(weight(w3_s), wide, NN) * f2_ref[n]
        for r in range(height):
            gp_ref[n, r + 1] = second[:, r * breadth : (r + 1) * breadth]
        halo_send(n, *g_args)
        eg_ref[...] += dot3((h2hi_ref[n], h2lo_ref[n]), wide, NT)

    def backward_two(n):
        halo_wait(n, *g_args)
        stack(n, gp_ref, gc_ref, thi_ref, tlo_ref, (2, 1, 0))
        taps = dot3(weight(wb_s), (thi_ref[...], tlo_ref[...]), NN)
        first = taps[0:mids, 2 * breadth : 2 * breadth + span]
        first = first + taps[mids : 2 * mids, breadth : breadth + span]
        first = first + taps[2 * mids : 3 * mids, 0:span]
        hi, lo = split(first * f1_ref[n])
        for r in range(height):
            at = slice(r * breadth, (r + 1) * breadth)
            out_ref[strided(n, r), :] = gj_ref[:, at] + dot3(
                weight(w1_s), (hi[:, at], lo[:, at]), NN
            )

        @pl.when(sec > 0)
        def _():
            relay(n, sec - 1).start()

        load_x(n)
        rg_ref[...] += dot3((wide_hi[...], wide_lo[...]), (hi, lo), NT)
        center = slice(mids, 2 * mids)
        grad = (thi_ref[center, breadth : breadth + span], tlo_ref[center, breadth : breadth + span])
        for a in range(3):
            at = slice(a * breadth, a * breadth + span)
            sg_ref[a] += dot3((shi_ref[n, :, at], slo_ref[n, :, at]), grad, NT)

    forward_one(0)
    forward_two(0)

    for n in range(images):
        backward_one(n)
        if n + 1 < images:
            forward_one(n + 1)
        backward_two(n)
        if n + 1 < images:
            forward_two(n + 1)

    for n in range(images):
        halo_drain(n, *h_args)
        halo_drain(n, *g_args)

        @pl.when(sec > 0)
        def _():
            relay(n, sec - 1).wait_send()


def per_device(
    block_input,
    grad_out,
    w_reduce,
    w_spatial,
    w_expand,
    scale_one,
    shift_one,
    scale_two,
    shift_two,
    scale_three,
    shift_three,
):
    sections, rows, cols = (lax.axis_size(a) for a in ("section", "row", "col"))
    _, images, chans, height, breadth = block_input.shape
    mids = w_reduce.shape[2]
    span = height * breadth
    wide = (height + 2) * breadth
    factor = 1.0 / jnp.sqrt(F32(images * span * rows * cols))
    sizes = (sections, rows, cols, images, height, breadth, chans, mids)
    x = block_input.reshape(images * chans * height, breadth)
    go = grad_out.reshape(images * chans * height, breadth)
    ws = w_spatial[0]
    wf = ws.transpose(0, 3, 1, 2).reshape(3 * mids, 3 * mids)
    wb = ws.transpose(0, 2, 1, 3).reshape(3 * mids, 3 * mids)
    small = jnp.stack([scale_one[0], shift_one[0], scale_two[0], shift_two[0]], axis=1)
    large = jnp.stack([scale_three[0], shift_three[0]], axis=1)
    w1 = w_reduce[0]
    w3 = w_expand[0]
    vmem = pl.BlockSpec(memory_space=pltpu.VMEM)
    pads = pltpu.VMEM((images, height + 2, mids, breadth), F32)
    packs = pltpu.VMEM((images, 2, 3, mids, breadth), F32)
    keeps = pltpu.VMEM((images, 2, mids, breadth), F32)
    out, rg, sg, eg = pl.pallas_call(
        functools.partial(kernel, sizes),
        out_shape=(
            jax.ShapeDtypeStruct(x.shape, F32),
            jax.ShapeDtypeStruct((chans, mids), F32),
            jax.ShapeDtypeStruct((3, 3 * mids, mids), F32),
            jax.ShapeDtypeStruct((mids, chans), F32),
        ),
        in_specs=[vmem, pl.BlockSpec(memory_space=pl.ANY)] + [vmem] * 8,
        out_specs=(vmem,) * 4,
        scratch_shapes=[
            pltpu.VMEM(x.shape, F32),
            pltpu.VMEM((images, chans, span), F32),
            pads,
            pads,
            packs,
            packs,
            keeps,
            keeps,
            pltpu.VMEM((images, 3 * mids, wide), BF16),
            pltpu.VMEM((images, 3 * mids, wide), BF16),
            pltpu.VMEM((3 * mids, wide), BF16),
            pltpu.VMEM((3 * mids, wide), BF16),
            pltpu.VMEM((images, mids, span), F32),
            pltpu.VMEM((images, mids, span), F32),
            pltpu.VMEM((images, mids, span), BF16),
            pltpu.VMEM((images, mids, span), BF16),
            pltpu.VMEM((chans, span), F32),
            pltpu.VMEM((chans, span), BF16),
            pltpu.VMEM((chans, span), BF16),
            pltpu.VMEM((2, mids, chans), BF16),
            pltpu.VMEM((2, chans, mids), BF16),
            pltpu.VMEM((2, 3 * mids, 3 * mids), BF16),
            pltpu.VMEM((2, 3 * mids, 3 * mids), BF16),
            pltpu.VMEM((2, chans, mids), BF16),
            pltpu.VMEM((2, mids, chans), BF16),
        ]
        + [pltpu.SemaphoreType.DMA((images, len(DIRS)))] * 4
        + [pltpu.SemaphoreType.DMA((images,))] * 3,
        compiler_params=pltpu.CompilerParams(
            collective_id=0, has_side_effects=True, vmem_limit_bytes=50 * 1024 * 1024
        ),
    )(x, go, w1.T, w1, wf, wb, w3.T, w3, small, large)
    rg, sg, eg = lax.psum((rg, sg, eg), ("row", "col"))
    return (
        out.reshape(block_input.shape),
        (rg * factor)[None],
        (sg * factor).reshape(w_spatial.shape),
        (eg * factor)[None],
    )


def solution(mesh):
    placed = (
        P("section", None, None, "row", "col"),
        P(None, None, "row", "col"),
        P("section", None, None),
        P("section", None, None, None, None),
        P("section", None, None),
        P("section", None),
        P("section", None),
        P("section", None),
        P("section", None),
        P("section", None),
        P("section", None),
    )
    return jax.shard_map(
        per_device,
        mesh=mesh,
        in_specs=placed,
        out_specs=(
            P("section", None, None, "row", "col"),
            P("section", None, None),
            P("section", None, None, None, None),
            P("section", None, None),
        ),
        check_vma=False,
    )
```
